32 devices in a mesh: shard: 8 (over z, y), tensor: 4 (over x, core).
Axes of the slice: x: 2, y: 2, z: 4, core: 2. Of those that a mesh axis runs over, the one named last changes fastest.
Arguments:
- big_grad: bfloat16 [2, 1280, 768], P(None, 'shard', 'tensor')
- big_weight: bfloat16 [2, 1280, 768], P(None, 'shard', 'tensor'), may hold values from -0.017944336 to 0.017944336
- big_moment: float32 [8, 768, 1280], P('shard', 'tensor'), may hold values from -6 to 6
- small_grad: bfloat16 [2, 1280, 192], P(None, 'shard')
- small_weight: bfloat16 [2, 1280, 192], P(None, 'shard'), may hold values from -0.15625 to 0.15625
- small_moment: float32 [8, 192, 1280], P('shard'), may hold values from -6 to 6
- owners: int32 [2, 2], replicated, may hold values from 0 to 7, as said below
- vec_parts: float32 [8, 2688], P('shard'), may hold values from -0.6 to 0.6
- vec_param: float32 [2688], P('shard'), may hold values from 0.5 to 1.5
- vec_first: float32 [2688], P('shard'), may hold values from -0.6 to 0.6
- vec_second: float32 [2688], P('shard'), may hold values from 0.01 to 1
Outputs:
- big_weight_new: bfloat16 [2, 1280, 768], P(None, 'shard', 'tensor')
- big_moment_new: float32 [8, 768, 1280], P('shard', 'tensor')
- small_weight_new: bfloat16 [2, 1280, 192], P(None, 'shard')
- small_moment_new: float32 [8, 192, 1280], P('shard')
- vec_param_new: float32 [2688], P('shard')
- vec_first_new: float32 [2688], P('shard')
- vec_second_new: float32 [2688], P('shard')
The draws below stay inside these ranges and needn't reach their ends.
Inputs may be any that keep to these rules, and one draw needn't show every extreme that they name: `owners`: no shard index appears twice in the whole list (over both rows); each aligned group of four shard indices holds exactly one owner of each row; the first and the last shard index own a matrix.
All inputs are finite; a program needn't handle non-finite values.
Results may differ from the reference program's by a relative error of at most 0.0068.
Values may be sent and summed in bfloat16 or wider, within the bound.
A program may use at most 64 MiB of HBM per device.

```python
import math
import jax
import jax.numpy as jnp
from jax import lax

D = 1280
ITERS = 2
QW = 768
KVW = 192
BIG = 2
VEC = 2688
N_SHARD = 8


def scaled_field(key, shape):
    first_key = jax.random.fold_in(key, 1)
    second_key = jax.random.fold_in(key, 2)
    third_key = jax.random.fold_in(key, 3)
    base = jnp.clip(jax.random.normal(first_key, shape, jnp.float32), -4.0, 4.0)
    row_scale = 10.0 ** jax.random.uniform(second_key, (shape[0], shape[1], 1), jnp.float32, -0.5, 0.5)
    column_scale = 10.0 ** jax.random.uniform(third_key, (shape[0], 1, shape[2]), jnp.float32, -0.5, 0.5)
    return base * row_scale * column_scale


def layered_field(key, shape):
    matrices = shape[0]
    strong_terms = 16
    medium_terms = 48
    terms = strong_terms + medium_terms
    left_int = jax.random.randint(jax.random.fold_in(key, 41), (matrices, shape[1], terms), -128, 129).astype(jnp.int32)
    strong_amp = jax.random.randint(jax.random.fold_in(key, 42), (matrices, strong_terms, 1), 96, 129).astype(jnp.int32)
    medium_amp = jax.random.randint(jax.random.fold_in(key, 43), (matrices, medium_terms, 1), 40, 57).astype(jnp.int32)
    amplitude = jnp.concatenate([strong_amp, medium_amp], axis=1)
    right_unit = jax.random.randint(jax.random.fold_in(key, 44), (matrices, terms, shape[2]), -128, 129).astype(jnp.int32)
    right_int = right_unit * amplitude // 128
    product = lax.dot_general(left_int.astype(jnp.float32), right_int.astype(jnp.float32), (((2,), (1,)), ((0,), (0,))), precision=lax.Precision.HIGHEST)
    low = product * 0.0001220703125
    column_scale = 10.0 ** jax.random.uniform(jax.random.fold_in(key, 46), (matrices, 1, shape[2]), jnp.float32, -0.5, 0.5)
    row_scale = 10.0 ** jax.random.uniform(jax.random.fold_in(key, 47), (matrices, shape[1], 1), jnp.float32, -0.5, 0.5)
    overall = 0.5
    return overall * low * row_scale * column_scale


def draw_big_grad(key, part):
    return layered_field(jax.random.fold_in(key, 11), (BIG, D, QW)).astype(jnp.bfloat16)


def draw_small_grad(key, part):
    return scaled_field(jax.random.fold_in(key, 13), (BIG, D, KVW)).astype(jnp.bfloat16)


def draw_owners(key, part):
    groups = BIG
    group_index = jnp.arange(groups, dtype=jnp.int32)
    first_offset = jax.random.randint(jax.random.fold_in(key, 31), (groups,), 0, 4).astype(jnp.int32)
    first_offset = jnp.where(group_index == 0, 0, jnp.where(group_index == groups - 1, 3, first_offset))
    step_offset = jax.random.randint(jax.random.fold_in(key, 32), (groups,), 1, 4).astype(jnp.int32)
    second_offset = (first_offset + step_offset) % 4
    first_order = jax.random.permutation(jax.random.fold_in(key, 33), groups).astype(jnp.int32)
    second_order = jax.random.permutation(jax.random.fold_in(key, 34), groups).astype(jnp.int32)
    first_row = first_order * 4 + jnp.take(first_offset, first_order)
    second_row = second_order * 4 + jnp.take(second_offset, second_order)
    return jnp.stack([first_row, second_row]).astype(jnp.int32)


def steps_of(own_key, extent, pieces, least, high):
    level, own = 1.0, jax.random.fold_in(own_key, 6)
    for dim, blocks in pieces:
        heights = jnp.exp(jax.random.uniform(jax.random.fold_in(own, dim), (blocks,), jnp.float32, least / len(pieces), high / len(pieces)))
        level = level * jnp.repeat(heights, extent[dim] // blocks).reshape([-1 if axis == dim else 1 for axis in range(len(extent))])
    return level


def normal_values(own_key, dims, deviation, most, shards=(), kind=jnp.bfloat16):
    entries = jax.random.normal(own_key, dims, jnp.float32) * deviation
    if len(shards) > 0:
        entries = steps_of(own_key, dims, shards, -0.22, 0.18) * entries
    return jnp.clip(entries, min=-most, max=most).astype(kind)


def setup_inputs(seed: int = 0) -> dict:
    arg_keys = jax.random.split(jax.random.key(seed), 12)
    return {
        "big_grad": draw_big_grad(jax.random.fold_in(arg_keys[11], 71), 0),
        "big_weight": normal_values(arg_keys[1], (BIG, D, QW), 0.003, 0.017944336, ((1, 8), (2, 4))),
        "big_moment": normal_values(arg_keys[2], (N_SHARD, QW, D), 1.0, 6.0, ((0, 8), (1, 4)), jnp.float32),
        "small_grad": draw_small_grad(jax.random.fold_in(arg_keys[11], 71), 0),
        "small_weight": normal_values(arg_keys[4], (BIG, D, KVW), D ** -0.5, 0.15625, ((1, 8),)),
        "small_moment": normal_values(arg_keys[5], (N_SHARD, KVW, D), 1.0, 6.0, ((0, 8),), jnp.float32),
        "owners": draw_owners(jax.random.fold_in(arg_keys[11], 71), 0),
        "vec_parts": normal_values(arg_keys[7], (N_SHARD, VEC), 0.1, 0.6, ((0, 8),), jnp.float32),
        "vec_param": jnp.clip(1.0 + 0.1 * jax.random.normal(arg_keys[8], (VEC,), jnp.float32), 0.5, 1.5),
        "vec_first": normal_values(arg_keys[9], (VEC,), 0.1, 0.6, ((0, 8),), jnp.float32),
        "vec_second": jnp.clip(jnp.exp(math.log(1.0) - 4.6051702 * jax.random.uniform(arg_keys[10], (VEC,), jnp.float32) ** steps_of(arg_keys[10], (VEC,), ((0, 8),), -0.2, 0.2)), 0.01, 1.0),
    }


newton_linear = 3.4445
newton_cubic = -4.775
newton_quintic = 2.0315
momentum_rate = 0.95
muon_rate = 0.05
weight_decay = 0.1
norm_epsilon = 1e-07
adam_rate = 0.004
first_decay = 0.9
second_decay = 0.95
adam_epsilon = 1e-08
first_correct = 0.99997343860111
second_correct = 0.99407947077967

def normalized(field):
    values = field.astype(jnp.float32)
    squares = jnp.sum(values * values)
    return (values / (jnp.sqrt(squares) + norm_epsilon)).astype(jnp.bfloat16)

def gram_block(left_part, right_part):
    product = lax.dot_general(left_part.astype(jnp.float32), right_part.astype(jnp.float32), (((0,), (0,)), ((), ())))
    return product.astype(jnp.bfloat16)

def poly_block(gram_part, gram_full):
    square = jnp.dot(gram_part, gram_full, preferred_element_type=jnp.float32)
    return (newton_cubic * gram_part.astype(jnp.float32) + newton_quintic * square).astype(jnp.bfloat16)

def newton_step(column_part, full_iterate, polynomial):
    product = lax.dot_general(full_iterate.astype(jnp.float32), polynomial.astype(jnp.float32), (((1,), (1,)), ((), ())))
    return (newton_linear * column_part.astype(jnp.float32) + product).astype(jnp.bfloat16)

def orthogonal(field):
    iterate = normalized(field)
    for iteration in range(ITERS):
        gram_full = gram_block(iterate, iterate)
        iterate = newton_step(iterate, iterate, poly_block(gram_full, gram_full))
    return iterate

def apply_update(weight, update):
    scale = 0.2 * math.sqrt(D)
    values = weight.astype(jnp.float32)
    return (values - muon_rate * (scale * update.astype(jnp.float32) + weight_decay * values)).astype(jnp.bfloat16)

def update_kind(gradients, weights, moments, owner_indices):

    def update_one(packed):
        gradient, weight, owner_index = packed
        previous = lax.dynamic_index_in_dim(moments, owner_index.astype(jnp.int32), 0, keepdims=False).T
        values = gradient.astype(jnp.float32)
        renewed = momentum_rate * previous + values
        blended = (values + momentum_rate * renewed).astype(jnp.bfloat16)
        return (apply_update(weight, orthogonal(blended)), renewed)
    new_weights, renewed_all = lax.map(update_one, (gradients, weights, owner_indices))
    new_moments = moments.at[owner_indices.astype(jnp.int32)].set(jnp.swapaxes(renewed_all, 1, 2))
    return (new_weights, new_moments)

def reference(big_grad, big_weight, big_moment, small_grad, small_weight, small_moment, owners, vec_parts, vec_param, vec_first, vec_second):
    big_weight_new, big_moment_new = update_kind(big_grad, big_weight, big_moment, owners[0])
    small_weight_new, small_moment_new = update_kind(small_grad, small_weight, small_moment, owners[1])
    gain_grad = lax.optimization_barrier(jnp.sum(vec_parts, axis=0))
    first_new = first_decay * vec_first + (1.0 - first_decay) * gain_grad
    second_new = second_decay * vec_second + (1.0 - second_decay) * gain_grad * gain_grad
    param_new = vec_param - adam_rate * (first_new / first_correct) / (jnp.sqrt(second_new / second_correct) + adam_epsilon)
    return (big_weight_new, big_moment_new, small_weight_new, small_moment_new, param_new, first_new, second_new)
```

```python
import math

import jax
import jax.numpy as jnp
from jax import lax
from jax.experimental import pallas as pl
from jax.experimental.pallas import tpu as pltpu
from jax.sharding import PartitionSpec as P

D = 1280
ITERS = 2


newton_linear = 3.4445
newton_cubic = -4.775
newton_quintic = 2.0315
momentum_rate = 0.95
muon_rate = 0.05
weight_decay = 0.1
norm_epsilon = 1e-07
adam_rate = 0.004
first_decay = 0.9
second_decay = 0.95
adam_epsilon = 1e-08
first_correct = 0.99997343860111
second_correct = 0.99407947077967


def owner_table(owner_list, count):
    devices = lax.broadcasted_iota(jnp.int32, (count, owner_list.shape[0]), 0)
    return (devices == owner_list[None, :]).astype(jnp.bfloat16)


def route_rows(owner_map, pieces):
    flattened = pieces.reshape(pieces.shape[0], -1)
    routed = jnp.dot(owner_map, flattened, preferred_element_type=jnp.float32)
    return routed.astype(jnp.bfloat16).reshape((owner_map.shape[0],) + pieces.shape[1:])


def collect(owner_map, arrived):
    flattened = arrived.reshape(arrived.shape[0], -1)
    picked = lax.dot_general(
        owner_map, flattened, (((0,), (0,)), ((), ())), preferred_element_type=jnp.float32
    )
    return picked.astype(jnp.bfloat16).reshape((owner_map.shape[1],) + arrived.shape[1:])


def advance(arrived, moment, is_owner):
    gradient = arrived.T.astype(jnp.float32)
    renewed = momentum_rate * moment + gradient
    retained = jnp.where(is_owner, renewed, moment)
    blended = jnp.where(is_owner, gradient + momentum_rate * renewed, 0.0).astype(jnp.bfloat16).T
    return (retained, blended)


def normalized(field):
    values = field.astype(jnp.float32)
    squares = jnp.sum(values * values)
    return (values / (jnp.sqrt(squares) + norm_epsilon)).astype(jnp.bfloat16)


def gram_block(left_part, right_part):
    product = lax.dot_general(
        left_part, right_part, (((0,), (0,)), ((), ())), preferred_element_type=jnp.float32
    )
    return product.astype(jnp.bfloat16)


def poly_block(gram_part, gram_full):
    square = jnp.dot(gram_part, gram_full, preferred_element_type=jnp.float32)
    return (newton_cubic * gram_part.astype(jnp.float32) + newton_quintic * square).astype(
        jnp.bfloat16
    )


def newton_step(column_part, full_iterate, polynomial):
    product = lax.dot_general(
        full_iterate, polynomial, (((1,), (1,)), ((), ())), preferred_element_type=jnp.float32
    )
    return (newton_linear * column_part.astype(jnp.float32) + product).astype(jnp.bfloat16)


def small_newton(field):
    iterate = normalized(field)
    for iteration in range(ITERS):
        gram_full = gram_block(iterate, iterate)
        iterate = newton_step(iterate, iterate, poly_block(gram_full, gram_full))
    return iterate


def apply_update(weight, update):
    scale = 0.2 * math.sqrt(D)
    values = weight.astype(jnp.float32)
    return (
        values - muon_rate * (scale * update.astype(jnp.float32) + weight_decay * values)
    ).astype(jnp.bfloat16)


def gather_columns(column_part):
    return lax.all_gather(column_part, "tensor", axis=1, tiled=True)


def gather_gram(gram_part):
    return lax.all_gather(gram_part, "tensor", axis=0, tiled=True)


def per_device_routed(
    big_grad,
    big_weight,
    big_moment,
    small_grad,
    small_weight,
    small_moment,
    owners,
    vec_parts,
    vec_param,
    vec_first,
    vec_second,
):
    shards = lax.axis_size("shard")
    shard_place = lax.axis_index("shard")
    column = lax.axis_index("tensor")
    block_width = big_grad.shape[2]
    rows_dev = big_grad.shape[1]
    matrices = big_grad.shape[0]
    joint_map = owner_table(jnp.concatenate([owners[0], owners[1]]), shards)
    joint_pieces = jnp.concatenate([big_grad, small_grad], axis=0)
    arrived = lax.all_to_all(
        route_rows(joint_map, joint_pieces), "shard", split_axis=0, concat_axis=1, tiled=True
    )[0]
    big_owner = jnp.any(owners[0] == shard_place)
    small_owner = jnp.any(owners[1] == shard_place)
    big_retained, big_blended = advance(arrived, big_moment[0], big_owner)
    small_retained, small_blended = advance(arrived, small_moment[0], small_owner)
    small_result = small_newton(small_blended)
    full_iterate = normalized(gather_columns(big_blended))
    for iteration in range(ITERS):
        owned_part = lax.dynamic_slice_in_dim(full_iterate, column * block_width, block_width, 1)
        gram_full = gather_gram(gram_block(owned_part, full_iterate))
        full_iterate = newton_step(full_iterate, full_iterate, poly_block(gram_full, gram_full))
    big_result = lax.dynamic_slice_in_dim(full_iterate, column * block_width, block_width, 1)
    own_result = jnp.where(big_owner, big_result, small_result)
    returned = lax.all_to_all(
        own_result.reshape(shards, rows_dev, block_width),
        "shard",
        split_axis=0,
        concat_axis=0,
        tiled=True,
    )
    picked = collect(joint_map, returned)
    big_weight_new = apply_update(big_weight, picked[:matrices])
    small_weight_new = apply_update(small_weight, picked[matrices:])
    grad_share = lax.psum_scatter(vec_parts[0], "shard", scatter_dimension=0, tiled=True)
    first_new = first_decay * vec_first + (1.0 - first_decay) * grad_share
    second_new = second_decay * vec_second + (1.0 - second_decay) * grad_share * grad_share
    param_new = vec_param - adam_rate * (first_new / first_correct) / (
        jnp.sqrt(second_new / second_correct) + adam_epsilon
    )
    return (
        big_weight_new,
        big_retained[None],
        small_weight_new,
        small_retained[None],
        param_new,
        first_new,
        second_new,
    )


ROWS = 160
BIG_W = 192
SMALL_W = 48
BLOCK = BIG_W + SMALL_W
PART = 80
LANES = 384
ORDERS = (("x", "y", "z"), ("y", "z", "x"), ("z", "x", "y"))
MESH = pl.DeviceIdType.MESH


def nt_dot(left, right):
    return lax.dot_general(left, right, (((1,), (1,)), ((), ())), preferred_element_type=jnp.float32)


def trace_of(gram_ref):
    width = gram_ref.shape[0]
    step = 64
    total = jnp.zeros((step, step), jnp.float32)
    for start in range(0, width, 128):
        size = min(128, width - start)
        piece = gram_ref[start : start + size, start : start + size]
        row = lax.broadcasted_iota(jnp.int32, (size, size), 0)
        col = lax.broadcasted_iota(jnp.int32, (size, size), 1)
        kept = jnp.where(row == col, piece, 0.0)
        total = total + jnp.sum(kept)
    return total[0:1, 0:1]


def first_step(x_ref, gram_f32, gram_ref, poly_ref, out_ref):
    width = x_ref.shape[0]
    tile = min(256, width)
    for n in range(0, width, tile):
        gram_f32[:, n : n + tile] = nt_dot(x_ref[...], x_ref[n : n + tile, :])
    squares = trace_of(gram_f32)
    inverse = 1.0 / (jnp.sqrt(squares) + norm_epsilon)
    gram_ref[...] = (gram_f32[...] * (inverse * inverse)).astype(jnp.bfloat16)
    for n in range(0, width, tile):
        square = jnp.dot(gram_ref[...], gram_ref[:, n : n + tile], preferred_element_type=jnp.float32)
        poly_ref[:, n : n + tile] = (
            newton_cubic * gram_ref[:, n : n + tile].astype(jnp.float32) + newton_quintic * square
        ).astype(jnp.bfloat16)
    for n in range(0, x_ref.shape[1], 256):
        product = jnp.dot(poly_ref[...], x_ref[:, n : n + 256], preferred_element_type=jnp.float32)
        out_ref[:, n : n + 256] = (
            (newton_linear * x_ref[:, n : n + 256].astype(jnp.float32) + product) * inverse
        ).astype(jnp.bfloat16)


def last_step(x_ref, gram_ref, own, count, main_lanes, rest_lanes):
    width = x_ref.shape[0]
    tile = min(256, width)
    for n in range(0, width, tile):
        gram_ref[:, n : n + tile] = nt_dot(x_ref[...], x_ref[n : n + tile, :]).astype(jnp.bfloat16)
    part = gram_ref[own, :]
    square = jnp.dot(part, gram_ref[...], preferred_element_type=jnp.float32)
    poly = (newton_cubic * part.astype(jnp.float32) + newton_quintic * square).astype(jnp.bfloat16)
    results = []
    for lanes in (main_lanes, rest_lanes):
        product = jnp.dot(poly, x_ref[:, lanes], preferred_element_type=jnp.float32)
        results.append(newton_linear * x_ref[own, lanes].astype(jnp.float32) + product)
    return results


def muon_kernel(
    owners,
    big_grad,
    big_weight,
    big_moment,
    small_grad,
    small_weight,
    small_moment,
    parts,
    param,
    first,
    second,
    big_weight_new,
    big_moment_new,
    small_weight_new,
    small_moment_new,
    param_new,
    first_new,
    second_new,
    grad_rows,
    grad_out,
    moment_out,
    moment_in,
    blocks,
    big_x,
    big_next,
    small_x,
    small_next,
    big_gram_f32,
    big_gram,
    big_poly,
    small_gram_f32,
    small_gram,
    small_poly,
    result_rows,
    result_in,
    parts_in,
    swap_sem,
    moment_sem,
    stage_send,
    stage_recv,
    pair_send,
    pair_recv,
    own_sem,
    back_sem,
    vec_send,
    vec_recv,
):
    shard = lax.axis_index("shard")
    tensor = lax.axis_index("tensor")
    group = shard // 4
    place = shard % 4
    z, y = place // 2, shard % 2
    x, core = tensor // 2, tensor % 2
    partner = {"shard": (shard + 4) % 8, "tensor": tensor}
    sibling = {"shard": shard, "tensor": x * 2 + (1 - core)}
    neighbour = {
        "x": {"shard": shard, "tensor": (1 - x) * 2 + core},
        "y": {"shard": group * 4 + z * 2 + (1 - y), "tensor": tensor},
        "z": {"shard": group * 4 + (1 - z) * 2 + y, "tensor": tensor},
    }

    barrier = pltpu.get_barrier_semaphore()
    for k in range(1, 8):
        pl.semaphore_signal(
            barrier, inc=1, device_id={"shard": (shard + k) % 8, "tensor": tensor}, device_id_type=MESH
        )
    for peer in (neighbour["x"], sibling):
        pl.semaphore_signal(barrier, inc=1, device_id=peer, device_id_type=MESH)

    first_is_mine = jnp.where(owners[0, 0] >= 4, 1, 0) == group
    small_is_mine = jnp.where(owners[1, 0] >= 4, 1, 0) == group
    big_owner = lax.rem(jnp.where(first_is_mine, owners[0, 0], owners[0, 1]), 4)
    small_owner = lax.rem(jnp.where(small_is_mine, owners[1, 0], owners[1, 1]), 4)

    def columns(index):
        big = jnp.where(first_is_mine == (index == 0), big_grad[0].astype(jnp.float32), big_grad[1].astype(jnp.float32))
        small = jnp.where(
            small_is_mine == (index == 0), small_grad[0].astype(jnp.float32), small_grad[1].astype(jnp.float32)
        )
        picked = small[:, 0:SMALL_W]
        for k in range(1, 4):
            picked = jnp.where(tensor == k, small[:, k * SMALL_W : (k + 1) * SMALL_W], picked)
        filler = jnp.zeros((ROWS, 256 - BLOCK), jnp.float32)
        return jnp.concatenate([big, picked, filler], axis=1).astype(jnp.bfloat16)

    grad_out[...] = columns(1)
    pl.semaphore_wait(barrier, 9)
    own_rows = pl.ds(pl.multiple_of(group * ROWS, ROWS), ROWS)
    other_rows = pl.ds(pl.multiple_of((1 - group) * ROWS, ROWS), ROWS)
    swap = pltpu.make_async_remote_copy(
        grad_out, grad_rows.at[own_rows], swap_sem.at[0], swap_sem.at[1], device_id=partner, device_id_type=MESH
    )
    swap.start()

    moment = jnp.concatenate(
        [big_moment[0], small_moment[0, pl.ds(pl.multiple_of(tensor * SMALL_W, SMALL_W), SMALL_W), :]], axis=0
    )
    for j in range(4):
        moment_out[j] = jnp.concatenate(
            [
                moment[:, j * ROWS : (j + 1) * ROWS],
                moment[:, (j + 4) * ROWS : (j + 5) * ROWS],
                jnp.zeros((BLOCK, LANES - 2 * ROWS), jnp.float32),
            ],
            axis=1,
        ).astype(jnp.bfloat16)
    moves = []
    for k in (3, 2, 1):
        there = (place + k) % 4
        moves.append(
            pltpu.make_async_remote_copy(
                moment_out.at[there],
                moment_in.at[place],
                moment_sem.at[0, k],
                moment_sem.at[1, k],
                device_id={"shard": group * 4 + there, "tensor": tensor},
                device_id_type=MESH,
            )
        )
        moves[-1].start()
    vec_moves = []
    for k in range(1, 8):
        there = (shard + k) % 8
        vec_moves.append(
            pltpu.make_async_remote_copy(
                parts.at[there],
                parts_in.at[k],
                vec_send.at[k],
                vec_recv.at[k],
                device_id={"shard": there, "tensor": tensor},
                device_id_type=MESH,
            )
        )
        vec_moves[-1].start()
    moment_in[place] = moment_out[place]
    grad_rows[own_rows, :] = columns(0)
    grad_rows[2 * ROWS :, :] = jnp.zeros((LANES - 2 * ROWS, 256), jnp.bfloat16)
    swap.wait_recv()
    gradient = grad_rows[...].astype(jnp.float32).T[:BLOCK]
    for move in moves:
        move.wait_recv()
    previous = jnp.concatenate([moment_in[big_owner, :BIG_W, :], moment_in[small_owner, BIG_W:, :]], axis=0)
    renewed = momentum_rate * previous.astype(jnp.float32) + gradient
    blended = gradient + momentum_rate * renewed
    rest = blended[:, 256:]
    rest = jnp.where(y == 0, rest, pltpu.roll(rest, 64, 1))
    blocks[z, y, x, core, :, 0:256] = blended[:, :256].astype(jnp.bfloat16)
    blocks[z, y, x, core, :, 256:] = rest.astype(jnp.bfloat16)

    here = {"x": x, "y": y, "z": z}

    def region(p, k, received):
        done = ORDERS[p][:k]
        index = []
        for name in ("z", "y", "x"):
            if name in done:
                index.append(slice(None))
            elif received and name == ORDERS[p][k]:
                index.append(1 - here[name])
            else:
                index.append(here[name])
        return blocks.at[index[0], index[1], index[2], core, p * PART : (p + 1) * PART]

    def stage(p, k):
        ref = region(p, k, False)
        return pltpu.make_async_remote_copy(
            ref,
            ref,
            stage_send.at[p, k],
            stage_recv.at[p, k],
            device_id=neighbour[ORDERS[p][k]],
            device_id_type=MESH,
        )

    def forward(p, k):
        ref = region(p, k, True)
        return pltpu.make_async_remote_copy(
            ref, ref, pair_send.at[p, k], pair_recv.at[p, k], device_id=sibling, device_id_type=MESH
        )

    sent = []
    for p in range(3):
        copy = stage(p, 0)
        copy.start()
        sent.append(copy)
    own_ref = blocks.at[z, y, x, core]
    own_copy = pltpu.make_async_remote_copy(
        own_ref, own_ref, own_sem.at[0], own_sem.at[1], device_id=sibling, device_id_type=MESH
    )
    own_copy.start()
    forwarded = []
    for k in range(3):
        for p in range(3):
            sent[3 * k + p].wait_recv()
            if k < 2:
                copy = stage(p, k + 1)
                copy.start()
                sent.append(copy)
            copy = forward(p, k)
            copy.start()
            forwarded.append(copy)
    own_copy.wait_recv()
    for copy in forwarded:
        copy.wait_recv()

    for a in range(2):
        for b in range(2):
            lanes = slice((2 * a + b) * 256, (2 * a + b + 1) * 256)
            for t in range(4):
                big_x[t * BIG_W : (t + 1) * BIG_W, lanes] = blocks[a, b, t // 2, t % 2, :BIG_W, :256]
                small_x[t * SMALL_W : (t + 1) * SMALL_W, lanes] = blocks[a, b, t // 2, t % 2, BIG_W:, :256]
        lanes = slice(1024 + a * 128, 1024 + (a + 1) * 128)
        for t in range(4):
            both = blocks[a, 0, t // 2, t % 2, :, 256:] + blocks[a, 1, t // 2, t % 2, :, 256:]
            big_x[t * BIG_W : (t + 1) * BIG_W, lanes] = both[:BIG_W]
            small_x[t * SMALL_W : (t + 1) * SMALL_W, lanes] = both[BIG_W:]

    first_step(small_x, small_gram_f32, small_gram, small_poly, small_next)
    first_step(big_x, big_gram_f32, big_gram, big_poly, big_next)
    main_lanes = pl.ds(pl.multiple_of(place * 256, 256), 256)
    rest_lanes = pl.ds(pl.multiple_of(1024 + z * 128, 128), 128)
    small_main, small_rest = last_step(
        small_next, small_gram, slice(None), 4 * SMALL_W, main_lanes, rest_lanes
    )
    own_columns = pl.ds(pl.multiple_of(tensor * BIG_W, BIG_W), BIG_W)
    big_main, big_rest = last_step(big_next, big_gram, own_columns, BIG_W, main_lanes, rest_lanes)
    main = jnp.concatenate([big_main, small_main], axis=0)
    rest = jnp.concatenate([big_rest, small_rest], axis=0)
    rest = jnp.where(y == 0, rest, pltpu.roll(rest, 64, 1))
    result_rows[0:256, :] = main.T.astype(jnp.bfloat16)
    result_rows[256:LANES, :] = rest.T.astype(jnp.bfloat16)
    back = pltpu.make_async_remote_copy(
        result_rows.at[other_rows], result_in, back_sem.at[0], back_sem.at[1], device_id=partner, device_id_type=MESH
    )
    back.start()

    share = parts[shard]
    for k in range(1, 8):
        vec_moves[k - 1].wait_recv()
        share = share + parts_in[k]
    first_value = first_decay * first[...] + (1.0 - first_decay) * share
    second_value = second_decay * second[...] + (1.0 - second_decay) * share * share
    first_new[...] = first_value
    second_new[...] = second_value
    param_new[...] = param[...] - adam_rate * (first_value / first_correct) / (
        jnp.sqrt(second_value / second_correct) + adam_epsilon
    )

    from_blended = 1.0 / (1.0 + momentum_rate)
    from_moment = momentum_rate - momentum_rate * momentum_rate / (1.0 + momentum_rate)

    def row_order(load):
        low, high = [], []
        for j in range(4):
            main = load(j // 2, j % 2, slice(0, 256)).astype(jnp.float32)
            rest = load(j // 2, j % 2, slice(256, LANES)).astype(jnp.float32)
            if j % 2 == 1:
                rest = pltpu.roll(rest, 64, 1)
            low.append(main[:, :ROWS])
            high.append(jnp.concatenate([main[:, ROWS:], rest[:, :64]], axis=1))
        return jnp.concatenate(low + high, axis=1)

    def small_block(a, b, lanes):
        return jnp.concatenate([blocks[a, b, t // 2, t % 2, BIG_W:, lanes] for t in range(4)], axis=0)

    big_blended = row_order(lambda a, b, lanes: blocks[a, b, x, core, :BIG_W, lanes])
    big_moment_new[0] = jnp.where(
        big_owner == place, from_blended * big_blended + from_moment * big_moment[0], big_moment[0]
    )
    small_blended = row_order(small_block)
    small_moment_new[0] = jnp.where(
        small_owner == place, from_blended * small_blended + from_moment * small_moment[0], small_moment[0]
    )

    back.wait_recv()
    mine = result_rows[own_rows, :]
    others = result_in[...]
    scale = 0.2 * math.sqrt(D)
    for index in range(2):
        for weight, out, lanes, is_mine in (
            (big_weight, big_weight_new, slice(0, BIG_W), first_is_mine),
            (small_weight, small_weight_new, slice(BIG_W, 2 * BIG_W), small_is_mine),
        ):
            update = jnp.where(
                is_mine == (index == 0), mine[:, lanes].astype(jnp.float32), others[:, lanes].astype(jnp.float32)
            )
            values = weight[index].astype(jnp.float32)
            out[index] = (values - muon_rate * (scale * update + weight_decay * values)).astype(jnp.bfloat16)
    for copy in [swap, own_copy, back] + moves + vec_moves + sent + forwarded:
        copy.wait_send()


def per_device(
    big_grad,
    big_weight,
    big_moment,
    small_grad,
    small_weight,
    small_moment,
    owners,
    vec_parts,
    vec_param,
    vec_first,
    vec_second,
):
    entries = vec_param.shape[0]
    shards = lax.axis_size("shard")
    vmem = pl.BlockSpec(memory_space=pltpu.VMEM)
    rows = jax.ShapeDtypeStruct((1, entries), jnp.float32)
    out_shape = (
        jax.ShapeDtypeStruct(big_weight.shape, jnp.bfloat16),
        jax.ShapeDtypeStruct(big_moment.shape, jnp.float32),
        jax.ShapeDtypeStruct(small_weight.shape, jnp.bfloat16),
        jax.ShapeDtypeStruct(small_moment.shape, jnp.float32),
        rows,
        rows,
        rows,
    )
    bf16, f32 = jnp.bfloat16, jnp.float32
    big, small = 4 * BIG_W, 4 * SMALL_W
    dma = pltpu.SemaphoreType.DMA
    outs = pl.pallas_call(
        muon_kernel,
        out_shape=out_shape,
        in_specs=[pl.BlockSpec(memory_space=pltpu.SMEM)] + [vmem] * 10,
        out_specs=(vmem,) * 7,
        scratch_shapes=[
            pltpu.VMEM((LANES, 256), bf16),
            pltpu.VMEM((ROWS, 256), bf16),
            pltpu.VMEM((4, BLOCK, LANES), bf16),
            pltpu.VMEM((4, BLOCK, LANES), bf16),
            pltpu.VMEM((2, 2, 2, 2, BLOCK, LANES), bf16),
            pltpu.VMEM((big, D), bf16),
            pltpu.VMEM((big, D), bf16),
            pltpu.VMEM((small, D), bf16),
            pltpu.VMEM((small, D), bf16),
            pltpu.VMEM((big, big), f32),
            pltpu.VMEM((big, big), bf16),
            pltpu.VMEM((big, big), bf16),
            pltpu.VMEM((small, small), f32),
            pltpu.VMEM((small, small), bf16),
            pltpu.VMEM((small, small), bf16),
            pltpu.VMEM((LANES, LANES), bf16),
            pltpu.VMEM((ROWS, LANES), bf16),
            pltpu.VMEM((shards, 1, entries), f32),
            dma((2,)),
            dma((2, 4)),
            dma((3, 3)),
            dma((3, 3)),
            dma((3, 3)),
            dma((3, 3)),
            dma((2,)),
            dma((2,)),
            dma((8,)),
            dma((8,)),
        ],
        compiler_params=pltpu.CompilerParams(
            collective_id=0, has_side_effects=True, vmem_limit_bytes=48 * 1024 * 1024
        ),
    )(
        owners,
        big_grad,
        big_weight,
        big_moment,
        small_grad,
        small_weight,
        small_moment,
        vec_parts.reshape(shards, 1, entries),
        vec_param.reshape(1, entries),
        vec_first.reshape(1, entries),
        vec_second.reshape(1, entries),
    )
    return tuple(outs[:4]) + tuple(value.reshape(entries) for value in outs[4:])


def solution(mesh):
    grouped = mesh.shape["shard"] == 8 and mesh.shape["tensor"] == 4
    return jax.shard_map(
        per_device if grouped else per_device_routed,
        mesh=mesh,
        in_specs=(
            P(None, "shard", "tensor"),
            P(None, "shard", "tensor"),
            P("shard", "tensor", None),
            P(None, "shard", None),
            P(None, "shard", None),
            P("shard", None, None),
            P(),
            P("shard", None),
            P("shard"),
            P("shard"),
            P("shard"),
        ),
        out_specs=(
            P(None, "shard", "tensor"),
            P("shard", "tensor", None),
            P(None, "shard", None),
            P("shard", None, None),
            P("shard"),
            P("shard"),
            P("shard"),
        ),
        check_vma=False,
    )
```

```python
import math

import jax
import jax.numpy as jnp
from jax import lax
from jax.experimental import pallas as pl
from jax.experimental.pallas import tpu as pltpu
from jax.sharding import PartitionSpec as P

D = 1280
ITERS = 2


newton_linear = 3.4445
newton_cubic = -4.775
newton_quintic = 2.0315
momentum_rate = 0.95
muon_rate = 0.05
weight_decay = 0.1
norm_epsilon = 1e-07
adam_rate = 0.004
first_decay = 0.9
second_decay = 0.95
adam_epsilon = 1e-08
first_correct = 0.99997343860111
second_correct = 0.99407947077967


def owner_table(owner_list, count):
    devices = lax.broadcasted_iota(jnp.int32, (count, owner_list.shape[0]), 0)
    return (devices == owner_list[None, :]).astype(jnp.bfloat16)


def route_rows(owner_map, pieces):
    flattened = pieces.reshape(pieces.shape[0], -1)
    routed = jnp.dot(owner_map, flattened, preferred_element_type=jnp.float32)
    return routed.astype(jnp.bfloat16).reshape((owner_map.shape[0],) + pieces.shape[1:])


def collect(owner_map, arrived):
    flattened = arrived.reshape(arrived.shape[0], -1)
    picked = lax.dot_general(
        owner_map, flattened, (((0,), (0,)), ((), ())), preferred_element_type=jnp.float32
    )
    return picked.astype(jnp.bfloat16).reshape((owner_map.shape[1],) + arrived.shape[1:])


def advance(arrived, moment, is_owner):
    gradient = arrived.T.astype(jnp.float32)
    renewed = momentum_rate * moment + gradient
    retained = jnp.where(is_owner, renewed, moment)
    blended = jnp.where(is_owner, gradient + momentum_rate * renewed, 0.0).astype(jnp.bfloat16).T
    return (retained, blended)


def normalized(field):
    values = field.astype(jnp.float32)
    squares = jnp.sum(values * values)
    return (values / (jnp.sqrt(squares) + norm_epsilon)).astype(jnp.bfloat16)


def gram_block(left_part, right_part):
    product = lax.dot_general(
        left_part, right_part, (((0,), (0,)), ((), ())), preferred_element_type=jnp.float32
    )
    return product.astype(jnp.bfloat16)


def poly_block(gram_part, gram_full):
    square = jnp.dot(gram_part, gram_full, preferred_element_type=jnp.float32)
    return (newton_cubic * gram_part.astype(jnp.float32) + newton_quintic * square).astype(
        jnp.bfloat16
    )


def newton_step(column_part, full_iterate, polynomial):
    product = lax.dot_general(
        full_iterate, polynomial, (((1,), (1,)), ((), ())), preferred_element_type=jnp.float32
    )
    return (newton_linear * column_part.astype(jnp.float32) + product).astype(jnp.bfloat16)


def small_newton(field):
    iterate = normalized(field)
    for iteration in range(ITERS):
        gram_full = gram_block(iterate, iterate)
        iterate = newton_step(iterate, iterate, poly_block(gram_full, gram_full))
    return iterate


def apply_update(weight, update):
    scale = 0.2 * math.sqrt(D)
    values = weight.astype(jnp.float32)
    return (
        values - muon_rate * (scale * update.astype(jnp.float32) + weight_decay * values)
    ).astype(jnp.bfloat16)


def gather_columns(column_part):
    return lax.all_gather(column_part, "tensor", axis=1, tiled=True)


def gather_gram(gram_part):
    return lax.all_gather(gram_part, "tensor", axis=0, tiled=True)


def per_device_routed(
    big_grad,
    big_weight,
    big_moment,
    small_grad,
    small_weight,
    small_moment,
    owners,
    vec_parts,
    vec_param,
    vec_first,
    vec_second,
):
    shards = lax.axis_size("shard")
    shard_place = lax.axis_index("shard")
    column = lax.axis_index("tensor")
    block_width = big_grad.shape[2]
    rows_dev = big_grad.shape[1]
    matrices = big_grad.shape[0]
    joint_map = owner_table(jnp.concatenate([owners[0], owners[1]]), shards)
    joint_pieces = jnp.concatenate([big_grad, small_grad], axis=0)
    arrived = lax.all_to_all(
        route_rows(joint_map, joint_pieces), "shard", split_axis=0, concat_axis=1, tiled=True
    )[0]
    big_owner = jnp.any(owners[0] == shard_place)
    small_owner = jnp.any(owners[1] == shard_place)
    big_retained, big_blended = advance(arrived, big_moment[0], big_owner)
    small_retained, small_blended = advance(arrived, small_moment[0], small_owner)
    small_result = small_newton(small_blended)
    full_iterate = normalized(gather_columns(big_blended))
    for iteration in range(ITERS):
        owned_part = lax.dynamic_slice_in_dim(full_iterate, column * block_width, block_width, 1)
        gram_full = gather_gram(gram_block(owned_part, full_iterate))
        full_iterate = newton_step(full_iterate, full_iterate, poly_block(gram_full, gram_full))
    big_result = lax.dynamic_slice_in_dim(full_iterate, column * block_width, block_width, 1)
    own_result = jnp.where(big_owner, big_result, small_result)
    returned = lax.all_to_all(
        own_result.reshape(shards, rows_dev, block_width),
        "shard",
        split_axis=0,
        concat_axis=0,
        tiled=True,
    )
    picked = collect(joint_map, returned)
    big_weight_new = apply_update(big_weight, picked[:matrices])
    small_weight_new = apply_update(small_weight, picked[matrices:])
    grad_share = lax.psum_scatter(vec_parts[0], "shard", scatter_dimension=0, tiled=True)
    first_new = first_decay * vec_first + (1.0 - first_decay) * grad_share
    second_new = second_decay * vec_second + (1.0 - second_decay) * grad_share * grad_share
    param_new = vec_param - adam_rate * (first_new / first_correct) / (
        jnp.sqrt(second_new / second_correct) + adam_epsilon
    )
    return (
        big_weight_new,
        big_retained[None],
        small_weight_new,
        small_retained[None],
        param_new,
        first_new,
        second_new,
    )


ROWS = 160
BIG_W = 192
SMALL_W = 48
BLOCK = BIG_W + SMALL_W
REST = 64
PACKED = BLOCK + REST
PARTS = ((0, 112), (112, 96), (208, 96))
LANES = 384
ORDERS = (("x", "y", "z"), ("y", "z", "x"), ("z", "x", "y"))
MESH = pl.DeviceIdType.MESH


def nt_dot(left, right):
    return lax.dot_general(left, right, (((1,), (1,)), ((), ())), preferred_element_type=jnp.float32)


def trace_of(gram_ref):
    width = gram_ref.shape[0]
    step = 64
    total = jnp.zeros((step, step), jnp.float32)
    for start in range(0, width, 128):
        size = min(128, width - start)
        piece = gram_ref[start : start + size, start : start + size]
        row = lax.broadcasted_iota(jnp.int32, (size, size), 0)
        col = lax.broadcasted_iota(jnp.int32, (size, size), 1)
        kept = jnp.where(row == col, piece, 0.0)
        total = total + jnp.sum(kept)
    return total[0:1, 0:1]


def first_step(x_ref, gram_f32, gram_ref, poly_ref, out_ref):
    width = x_ref.shape[0]
    tile = min(256, width)
    for n in range(0, width, tile):
        gram_f32[:, n : n + tile] = nt_dot(x_ref[...], x_ref[n : n + tile, :])
    squares = trace_of(gram_f32)
    inverse = 1.0 / (jnp.sqrt(squares) + norm_epsilon)
    gram_ref[...] = (gram_f32[...] * (inverse * inverse)).astype(jnp.bfloat16)
    for n in range(0, width, tile):
        square = jnp.dot(gram_ref[...], gram_ref[:, n : n + tile], preferred_element_type=jnp.float32)
        poly_ref[:, n : n + tile] = (
            newton_cubic * gram_ref[:, n : n + tile].astype(jnp.float32) + newton_quintic * square
        ).astype(jnp.bfloat16)
    for n in range(0, x_ref.shape[1], 256):
        product = jnp.dot(poly_ref[...], x_ref[:, n : n + 256], preferred_element_type=jnp.float32)
        out_ref[:, n : n + 256] = (
            (newton_linear * x_ref[:, n : n + 256].astype(jnp.float32) + product) * inverse
        ).astype(jnp.bfloat16)


def last_step(x_ref, gram_ref, own, count, main_lanes, rest_lanes):
    width = x_ref.shape[0]
    tile = min(256, width)
    for n in range(0, width, tile):
        gram_ref[:, n : n + tile] = nt_dot(x_ref[...], x_ref[n : n + tile, :]).astype(jnp.bfloat16)
    part = gram_ref[own, :]
    square = jnp.dot(part, gram_ref[...], preferred_element_type=jnp.float32)
    poly = (newton_cubic * part.astype(jnp.float32) + newton_quintic * square).astype(jnp.bfloat16)
    results = []
    for lanes in (main_lanes, rest_lanes):
        product = jnp.dot(poly, x_ref[:, lanes], preferred_element_type=jnp.float32)
        results.append(newton_linear * x_ref[own, lanes].astype(jnp.float32) + product)
    return results


def pack(block):
    groups = [block[k * REST : (k + 1) * REST, 256:320] for k in range(3)]
    groups.append(jnp.concatenate([block[BIG_W:, 256:320], jnp.zeros((REST - SMALL_W, 64), jnp.float32)], axis=0))
    return jnp.concatenate([block[:, :256], jnp.concatenate(groups, axis=1)], axis=0)


def muon_kernel(
    owners,
    big_grad_hbm,
    big_weight_hbm,
    big_moment_hbm,
    small_grad_hbm,
    small_weight_hbm,
    small_moment_hbm,
    parts_hbm,
    param,
    first,
    second,
    big_weight_new,
    big_moment_new,
    small_weight_new,
    small_moment_new,
    param_new,
    first_new,
    second_new,
    big_grad,
    big_weight,
    big_moment,
    small_grad,
    small_weight,
    small_moment,
    parts,
    load_sem,
    grad_rows,
    grad_out,
    moment_out,
    moment_in,
    blocks,
    big_x,
    big_next,
    small_x,
    small_next,
    big_gram_f32,
    big_gram,
    big_poly,
    small_gram_f32,
    small_gram,
    small_poly,
    result_rows,
    result_in,
    small_rows,
    small_in,
    parts_in,
    swap_sem,
    moment_sem,
    stage_send,
    stage_recv,
    pair_send,
    pair_recv,
    own_sem,
    back_sem,
    vec_send,
    vec_recv,
):
    loads = [
        pltpu.make_async_copy(source, target, load_sem.at[k])
        for k, (source, target) in enumerate(
            (
                (big_grad_hbm, big_grad),
                (small_grad_hbm, small_grad),
                (big_moment_hbm, big_moment),
                (small_moment_hbm, small_moment),
                (parts_hbm, parts),
                (big_weight_hbm, big_weight),
                (small_weight_hbm, small_weight),
            )
        )
    ]
    for copy in loads:
        copy.start()
    shard = lax.axis_index("shard")
    tensor = lax.axis_index("tensor")
    group = shard // 4
    place = shard % 4
    z, y = place // 2, shard % 2
    x, core = tensor // 2, tensor % 2
    partner = {"shard": (shard + 4) % 8, "tensor": tensor}
    sibling = {"shard": shard, "tensor": x * 2 + (1 - core)}
    neighbour = {
        "x": {"shard": shard, "tensor": (1 - x) * 2 + core},
        "y": {"shard": group * 4 + z * 2 + (1 - y), "tensor": tensor},
        "z": {"shard": group * 4 + (1 - z) * 2 + y, "tensor": tensor},
    }

    barrier = pltpu.get_barrier_semaphore()
    for k in range(1, 8):
        pl.semaphore_signal(
            barrier, inc=1, device_id={"shard": (shard + k) % 8, "tensor": tensor}, device_id_type=MESH
        )
    for peer in (neighbour["x"], sibling):
        pl.semaphore_signal(barrier, inc=1, device_id=peer, device_id_type=MESH)

    first_is_mine = jnp.where(owners[0, 0] >= 4, 1, 0) == group
    small_is_mine = jnp.where(owners[1, 0] >= 4, 1, 0) == group
    big_owner = lax.rem(jnp.where(first_is_mine, owners[0, 0], owners[0, 1]), 4)
    small_owner = lax.rem(jnp.where(small_is_mine, owners[1, 0], owners[1, 1]), 4)

    def columns(index):
        big = jnp.where(first_is_mine == (index == 0), big_grad[0].astype(jnp.float32), big_grad[1].astype(jnp.float32))
        small = jnp.where(
            small_is_mine == (index == 0), small_grad[0].astype(jnp.float32), small_grad[1].astype(jnp.float32)
        )
        picked = small[:, 0:SMALL_W]
        for k in range(1, 4):
            picked = jnp.where(tensor == k, small[:, k * SMALL_W : (k + 1) * SMALL_W], picked)
        filler = jnp.zeros((ROWS, 256 - BLOCK), jnp.float32)
        return jnp.concatenate([big, picked, filler], axis=1).astype(jnp.bfloat16)

    loads[0].wait()
    loads[1].wait()
    grad_out[...] = columns(1)
    pl.semaphore_wait(barrier, 9)
    own_rows = pl.ds(pl.multiple_of(group * ROWS, ROWS), ROWS)
    other_rows = pl.ds(pl.multiple_of((1 - group) * ROWS, ROWS), ROWS)
    swap = pltpu.make_async_remote_copy(
        grad_out, grad_rows.at[own_rows], swap_sem.at[0], swap_sem.at[1], device_id=partner, device_id_type=MESH
    )
    swap.start()

    loads[2].wait()
    loads[3].wait()
    moment = jnp.concatenate(
        [big_moment[0], small_moment[0, pl.ds(pl.multiple_of(tensor * SMALL_W, SMALL_W), SMALL_W), :]], axis=0
    )
    for j in range(4):
        rows = jnp.concatenate(
            [moment[:, j * ROWS : (j + 1) * ROWS], moment[:, (j + 4) * ROWS : (j + 5) * ROWS]], axis=1
        )
        moment_out[j] = pack(rows).astype(jnp.bfloat16)
    moves = []
    for k in (3, 2, 1):
        there = (place + k) % 4
        moves.append(
            pltpu.make_async_remote_copy(
                moment_out.at[there],
                moment_in.at[place],
                moment_sem.at[0, k],
                moment_sem.at[1, k],
                device_id={"shard": group * 4 + there, "tensor": tensor},
                device_id_type=MESH,
            )
        )
        moves[-1].start()
    loads[4].wait()
    vec_moves = []
    for k in range(1, 8):
        there = (shard + k) % 8
        vec_moves.append(
            pltpu.make_async_remote_copy(
                parts.at[there],
                parts_in.at[k],
                vec_send.at[k],
                vec_recv.at[k],
                device_id={"shard": there, "tensor": tensor},
                device_id_type=MESH,
            )
        )
        vec_moves[-1].start()
    moment_in[place] = moment_out[place]
    grad_rows[own_rows, :] = columns(0)
    grad_rows[2 * ROWS :, :] = jnp.zeros((LANES - 2 * ROWS, 256), jnp.bfloat16)
    swap.wait_recv()
    gradient = pack(grad_rows[...].astype(jnp.float32).T[:BLOCK])
    for move in moves:
        move.wait_recv()
    low = moment_in[big_owner, BLOCK:, :]
    high = moment_in[small_owner, BLOCK:, :]
    lane = lax.broadcasted_iota(jnp.int32, (REST, 256), 1)
    previous = jnp.concatenate(
        [
            moment_in[big_owner, :BIG_W, :].astype(jnp.float32),
            moment_in[small_owner, BIG_W:BLOCK, :].astype(jnp.float32),
            jnp.where(lane < BIG_W, low.astype(jnp.float32), high.astype(jnp.float32)),
        ],
        axis=0,
    )
    renewed = momentum_rate * previous + gradient
    blocks[z, y, x, core] = (gradient + momentum_rate * renewed).astype(jnp.bfloat16)

    here = {"x": x, "y": y, "z": z}

    def region(p, k, received):
        done = ORDERS[p][:k]
        index = []
        for name in ("z", "y", "x"):
            if name in done:
                index.append(slice(None))
            elif received and name == ORDERS[p][k]:
                index.append(1 - here[name])
            else:
                index.append(here[name])
        return blocks.at[index[0], index[1], index[2], core, pl.ds(*PARTS[p])]

    def stage(p, k):
        ref = region(p, k, False)
        return pltpu.make_async_remote_copy(
            ref,
            ref,
            stage_send.at[p, k],
            stage_recv.at[p, k],
            device_id=neighbour[ORDERS[p][k]],
            device_id_type=MESH,
        )

    def forward(p, k):
        ref = region(p, k, True)
        return pltpu.make_async_remote_copy(
            ref, ref, pair_send.at[p, k], pair_recv.at[p, k], device_id=sibling, device_id_type=MESH
        )

    sent = []
    for p in range(3):
        copy = stage(p, 0)
        copy.start()
        sent.append(copy)
    own_ref = blocks.at[z, y, x, core]
    own_copy = pltpu.make_async_remote_copy(
        own_ref, own_ref, own_sem.at[0], own_sem.at[1], device_id=sibling, device_id_type=MESH
    )
    own_copy.start()
    forwarded = []
    for k in range(3):
        for p in range(3):
            sent[3 * k + p].wait_recv()
            if k < 2:
                copy = stage(p, k + 1)
                copy.start()
                sent.append(copy)
            copy = forward(p, k)
            copy.start()
            forwarded.append(copy)
    own_copy.wait_recv()
    for copy in forwarded:
        copy.wait_recv()

    for a in range(2):
        for b in range(2):
            lanes = slice((2 * a + b) * 256, (2 * a + b + 1) * 256)
            for t in range(4):
                big_x[t * BIG_W : (t + 1) * BIG_W, lanes] = blocks[a, b, t // 2, t % 2, :BIG_W, :256]
                small_x[t * SMALL_W : (t + 1) * SMALL_W, lanes] = blocks[a, b, t // 2, t % 2, BIG_W:BLOCK, :256]
        lanes = slice(1024 + a * 128, 1024 + (a + 1) * 128)
        for t in range(4):
            left = blocks[a, 0, t // 2, t % 2, BLOCK:, :].astype(jnp.float32)
            right = blocks[a, 1, t // 2, t % 2, BLOCK:, :].astype(jnp.float32)
            for k in range(4):
                both = jnp.concatenate(
                    [left[:, k * 64 : (k + 1) * 64], right[:, k * 64 : (k + 1) * 64]], axis=1
                ).astype(jnp.bfloat16)
                if k < 3:
                    big_x[t * BIG_W + k * REST : t * BIG_W + (k + 1) * REST, lanes] = both
                else:
                    small_x[t * SMALL_W : (t + 1) * SMALL_W, lanes] = both[:SMALL_W]

    main_lanes = pl.ds(pl.multiple_of(place * 256, 256), 256)
    rest_lanes = pl.ds(pl.multiple_of(1024 + z * 128, 128), 128)

    def give_back(results, rows_ref, in_ref, sems):
        main, rest = results
        rest = jnp.where(y == 0, rest, pltpu.roll(rest, 64, 1))
        rows_ref[0:256, :] = main.T.astype(jnp.bfloat16)
        rows_ref[256:LANES, :] = rest.T.astype(jnp.bfloat16)
        copy = pltpu.make_async_remote_copy(
            rows_ref.at[other_rows], in_ref, sems.at[0], sems.at[1], device_id=partner, device_id_type=MESH
        )
        copy.start()
        return copy

    first_step(small_x, small_gram_f32, small_gram, small_poly, small_next)
    small_results = last_step(small_next, small_gram, slice(None), 4 * SMALL_W, main_lanes, rest_lanes)
    small_back = give_back(small_results, small_rows, small_in, back_sem.at[1])
    first_step(big_x, big_gram_f32, big_gram, big_poly, big_next)
    own_columns = pl.ds(pl.multiple_of(tensor * BIG_W, BIG_W), BIG_W)
    big_results = last_step(big_next, big_gram, own_columns, BIG_W, main_lanes, rest_lanes)
    back = give_back(big_results, result_rows, result_in, back_sem.at[0])

    share = parts[shard]
    for k in range(1, 8):
        vec_moves[k - 1].wait_recv()
        share = share + parts_in[k]
    first_value = first_decay * first[...] + (1.0 - first_decay) * share
    second_value = second_decay * second[...] + (1.0 - second_decay) * share * share
    first_new[...] = first_value
    second_new[...] = second_value
    param_new[...] = param[...] - adam_rate * (first_value / first_correct) / (
        jnp.sqrt(second_value / second_correct) + adam_epsilon
    )

    from_blended = 1.0 / (1.0 + momentum_rate)
    from_moment = momentum_rate - momentum_rate * momentum_rate / (1.0 + momentum_rate)

    def row_order(values):
        low, high = [], []
        for j in range(4):
            low.append(values[:, 256 * j : 256 * j + ROWS])
            high += [values[:, 256 * j + ROWS : 256 * (j + 1)], values[:, 1024 + 64 * j : 1024 + 64 * (j + 1)]]
        return jnp.concatenate(low + high, axis=1)

    big_moment_new[0] = jnp.where(
        big_owner == place,
        from_blended * row_order(big_x[own_columns, :].astype(jnp.float32)) + from_moment * big_moment[0],
        big_moment[0],
    )
    small_moment_new[0] = jnp.where(
        small_owner == place,
        from_blended * row_order(small_x[...].astype(jnp.float32)) + from_moment * small_moment[0],
        small_moment[0],
    )

    small_back.wait_recv()
    back.wait_recv()
    loads[5].wait()
    loads[6].wait()
    scale = 0.2 * math.sqrt(D)
    for index in range(2):
        for weight, out, rows_ref, in_ref, is_mine in (
            (small_weight, small_weight_new, small_rows, small_in, small_is_mine),
            (big_weight, big_weight_new, result_rows, result_in, first_is_mine),
        ):
            update = jnp.where(
                is_mine == (index == 0), rows_ref[own_rows, :].astype(jnp.float32), in_ref[...].astype(jnp.float32)
            )
            values = weight[index].astype(jnp.float32)
            out[index] = (values - muon_rate * (scale * update + weight_decay * values)).astype(jnp.bfloat16)
    for copy in [swap, own_copy, small_back, back] + moves + vec_moves + sent + forwarded:
        copy.wait_send()


def store_kernel(*refs):
    sems = refs[8]
    copies = [pltpu.make_async_copy(refs[k], refs[4 + k], sems.at[k]) for k in range(4)]
    for copy in copies:
        copy.start()
    for copy in copies:
        copy.wait()


def per_device(
    big_grad,
    big_weight,
    big_moment,
    small_grad,
    small_weight,
    small_moment,
    owners,
    vec_parts,
    vec_param,
    vec_first,
    vec_second,
):
    entries = vec_param.shape[0]
    shards = lax.axis_size("shard")
    vmem = pl.BlockSpec(memory_space=pltpu.VMEM)
    hbm = pl.BlockSpec(memory_space=pl.ANY)
    rows = jax.ShapeDtypeStruct((1, entries), jnp.float32)
    out_shape = (
        jax.ShapeDtypeStruct(big_weight.shape, jnp.bfloat16),
        jax.ShapeDtypeStruct(big_moment.shape, jnp.float32),
        jax.ShapeDtypeStruct(small_weight.shape, jnp.bfloat16),
        jax.ShapeDtypeStruct(small_moment.shape, jnp.float32),
        rows,
        rows,
        rows,
    )
    bf16, f32 = jnp.bfloat16, jnp.float32
    big, small = 4 * BIG_W, 4 * SMALL_W
    dma = pltpu.SemaphoreType.DMA
    outs = pl.pallas_call(
        muon_kernel,
        out_shape=out_shape,
        in_specs=[pl.BlockSpec(memory_space=pltpu.SMEM)] + [hbm] * 7 + [vmem] * 3,
        out_specs=(vmem,) * 7,
        scratch_shapes=[
            pltpu.VMEM(big_grad.shape, bf16),
            pltpu.VMEM(big_weight.shape, bf16),
            pltpu.VMEM(big_moment.shape, f32),
            pltpu.VMEM(small_grad.shape, bf16),
            pltpu.VMEM(small_weight.shape, bf16),
            pltpu.VMEM(small_moment.shape, f32),
            pltpu.VMEM((shards, 1, entries), f32),
            dma((7,)),
            pltpu.VMEM((LANES, 256), bf16),
            pltpu.VMEM((ROWS, 256), bf16),
            pltpu.VMEM((4, PACKED, 256), bf16),
            pltpu.VMEM((4, PACKED, 256), bf16),
            pltpu.VMEM((2, 2, 2, 2, PACKED, 256), bf16),
            pltpu.VMEM((big, D), bf16),
            pltpu.VMEM((big, D), bf16),
            pltpu.VMEM((small, D), bf16),
            pltpu.VMEM((small, D), bf16),
            pltpu.VMEM((big, big), f32),
            pltpu.VMEM((big, big), bf16),
            pltpu.VMEM((big, big), bf16),
            pltpu.VMEM((small, small), f32),
            pltpu.VMEM((small, small), bf16),
            pltpu.VMEM((small, small), bf16),
            pltpu.VMEM((LANES, BIG_W), bf16),
            pltpu.VMEM((ROWS, BIG_W), bf16),
            pltpu.VMEM((LANES, 4 * SMALL_W), bf16),
            pltpu.VMEM((ROWS, 4 * SMALL_W), bf16),
            pltpu.VMEM((shards, 1, entries), f32),
            dma((2,)),
            dma((2, 4)),
            dma((3, 3)),
            dma((3, 3)),
            dma((3, 3)),
            dma((3, 3)),
            dma((2,)),
            dma((2, 2)),
            dma((8,)),
            dma((8,)),
        ],
        compiler_params=pltpu.CompilerParams(
            collective_id=0, has_side_effects=True, vmem_limit_bytes=60 * 1024 * 1024
        ),
    )(
        owners,
        big_grad,
        big_weight,
        big_moment,
        small_grad,
        small_weight,
        small_moment,
        vec_parts.reshape(shards, 1, entries),
        vec_param.reshape(1, entries),
        vec_first.reshape(1, entries),
        vec_second.reshape(1, entries),
    )
    outs = list(outs)
    outs[:4] = pl.pallas_call(
        store_kernel,
        out_shape=out_shape[:4],
        in_specs=[pl.BlockSpec(memory_space=pl.ANY)] * 4,
        out_specs=(hbm,) * 4,
        scratch_shapes=[dma((4,))],
    )(*outs[:4])
    return tuple(outs[:4]) + tuple(value.reshape(entries) for value in outs[4:])


def solution(mesh):
    grouped = mesh.shape["shard"] == 8 and mesh.shape["tensor"] == 4
    return jax.shard_map(
        per_device if grouped else per_device_routed,
        mesh=mesh,
        in_specs=(
            P(None, "shard", "tensor"),
            P(None, "shard", "tensor"),
            P("shard", "tensor", None),
            P(None, "shard", None),
            P(None, "shard", None),
            P("shard", None, None),
            P(),
            P("shard", None),
            P("shard"),
            P("shard"),
            P("shard"),
        ),
        out_specs=(
            P(None, "shard", "tensor"),
            P("shard", "tensor", None),
            P(None, "shard", None),
            P("shard", None, None),
            P("shard"),
            P("shard"),
            P("shard"),
        ),
        check_vma=False,
    )
```

```python
import math

import jax
import jax.numpy as jnp
from jax import lax
from jax.experimental import pallas as pl
from jax.experimental.pallas import tpu as pltpu
from jax.sharding import PartitionSpec as P

D = 1280
ITERS = 2


newton_linear = 3.4445
newton_cubic = -4.775
newton_quintic = 2.0315
momentum_rate = 0.95
muon_rate = 0.05
weight_decay = 0.1
norm_epsilon = 1e-07
adam_rate = 0.004
first_decay = 0.9
second_decay = 0.95
adam_epsilon = 1e-08
first_correct = 0.99997343860111
second_correct = 0.99407947077967


def owner_table(owner_list, count):
    devices = lax.broadcasted_iota(jnp.int32, (count, owner_list.shape[0]), 0)
    return (devices == owner_list[None, :]).astype(jnp.bfloat16)


def route_rows(owner_map, pieces):
    flattened = pieces.reshape(pieces.shape[0], -1)
    routed = jnp.dot(owner_map, flattened, preferred_element_type=jnp.float32)
    return routed.astype(jnp.bfloat16).reshape((owner_map.shape[0],) + pieces.shape[1:])


def collect(owner_map, arrived):
    flattened = arrived.reshape(arrived.shape[0], -1)
    picked = lax.dot_general(
        owner_map, flattened, (((0,), (0,)), ((), ())), preferred_element_type=jnp.float32
    )
    return picked.astype(jnp.bfloat16).reshape((owner_map.shape[1],) + arrived.shape[1:])


def advance(arrived, moment, is_owner):
    gradient = arrived.T.astype(jnp.float32)
    renewed = momentum_rate * moment + gradient
    retained = jnp.where(is_owner, renewed, moment)
    blended = jnp.where(is_owner, gradient + momentum_rate * renewed, 0.0).astype(jnp.bfloat16).T
    return (retained, blended)


def normalized(field):
    values = field.astype(jnp.float32)
    squares = jnp.sum(values * values)
    return (values / (jnp.sqrt(squares) + norm_epsilon)).astype(jnp.bfloat16)


def gram_block(left_part, right_part):
    product = lax.dot_general(
        left_part, right_part, (((0,), (0,)), ((), ())), preferred_element_type=jnp.float32
    )
    return product.astype(jnp.bfloat16)


def poly_block(gram_part, gram_full):
    square = jnp.dot(gram_part, gram_full, preferred_element_type=jnp.float32)
    return (newton_cubic * gram_part.astype(jnp.float32) + newton_quintic * square).astype(
        jnp.bfloat16
    )


def newton_step(column_part, full_iterate, polynomial):
    product = lax.dot_general(
        full_iterate, polynomial, (((1,), (1,)), ((), ())), preferred_element_type=jnp.float32
    )
    return (newton_linear * column_part.astype(jnp.float32) + product).astype(jnp.bfloat16)


def small_newton(field):
    iterate = normalized(field)
    for iteration in range(ITERS):
        gram_full = gram_block(iterate, iterate)
        iterate = newton_step(iterate, iterate, poly_block(gram_full, gram_full))
    return iterate


def apply_update(weight, update):
    scale = 0.2 * math.sqrt(D)
    values = weight.astype(jnp.float32)
    return (
        values - muon_rate * (scale * update.astype(jnp.float32) + weight_decay * values)
    ).astype(jnp.bfloat16)


def gather_columns(column_part):
    return lax.all_gather(column_part, "tensor", axis=1, tiled=True)


def gather_gram(gram_part):
    return lax.all_gather(gram_part, "tensor", axis=0, tiled=True)


def per_device_routed(
    big_grad,
    big_weight,
    big_moment,
    small_grad,
    small_weight,
    small_moment,
    owners,
    vec_parts,
    vec_param,
    vec_first,
    vec_second,
):
    shards = lax.axis_size("shard")
    shard_place = lax.axis_index("shard")
    column = lax.axis_index("tensor")
    block_width = big_grad.shape[2]
    rows_dev = big_grad.shape[1]
    matrices = big_grad.shape[0]
    joint_map = owner_table(jnp.concatenate([owners[0], owners[1]]), shards)
    joint_pieces = jnp.concatenate([big_grad, small_grad], axis=0)
    arrived = lax.all_to_all(
        route_rows(joint_map, joint_pieces), "shard", split_axis=0, concat_axis=1, tiled=True
    )[0]
    big_owner = jnp.any(owners[0] == shard_place)
    small_owner = jnp.any(owners[1] == shard_place)
    big_retained, big_blended = advance(arrived, big_moment[0], big_owner)
    small_retained, small_blended = advance(arrived, small_moment[0], small_owner)
    small_result = small_newton(small_blended)
    full_iterate = normalized(gather_columns(big_blended))
    for iteration in range(ITERS):
        owned_part = lax.dynamic_slice_in_dim(full_iterate, column * block_width, block_width, 1)
        gram_full = gather_gram(gram_block(owned_part, full_iterate))
        full_iterate = newton_step(full_iterate, full_iterate, poly_block(gram_full, gram_full))
    big_result = lax.dynamic_slice_in_dim(full_iterate, column * block_width, block_width, 1)
    own_result = jnp.where(big_owner, big_result, small_result)
    returned = lax.all_to_all(
        own_result.reshape(shards, rows_dev, block_width),
        "shard",
        split_axis=0,
        concat_axis=0,
        tiled=True,
    )
    picked = collect(joint_map, returned)
    big_weight_new = apply_update(big_weight, picked[:matrices])
    small_weight_new = apply_update(small_weight, picked[matrices:])
    grad_share = lax.psum_scatter(vec_parts[0], "shard", scatter_dimension=0, tiled=True)
    first_new = first_decay * vec_first + (1.0 - first_decay) * grad_share
    second_new = second_decay * vec_second + (1.0 - second_decay) * grad_share * grad_share
    param_new = vec_param - adam_rate * (first_new / first_correct) / (
        jnp.sqrt(second_new / second_correct) + adam_epsilon
    )
    return (
        big_weight_new,
        big_retained[None],
        small_weight_new,
        small_retained[None],
        param_new,
        first_new,
        second_new,
    )


ROWS = 160
BIG_W = 192
SMALL_W = 48
BLOCK = BIG_W + SMALL_W
REST = 64
PACKED = BLOCK + REST
PARTS = ((0, 112), (112, 96), (208, 96))
LANES = 384
ORDERS = (("x", "y", "z"), ("y", "z", "x"), ("z", "x", "y"))
MESH = pl.DeviceIdType.MESH


def nt_dot(left, right):
    return lax.dot_general(left, right, (((1,), (1,)), ((), ())), preferred_element_type=jnp.float32)


def trace_of(gram_ref):
    width = gram_ref.shape[0]
    step = 64
    total = jnp.zeros((step, step), jnp.float32)
    for start in range(0, width, 128):
        size = min(128, width - start)
        piece = gram_ref[start : start + size, start : start + size]
        row = lax.broadcasted_iota(jnp.int32, (size, size), 0)
        col = lax.broadcasted_iota(jnp.int32, (size, size), 1)
        kept = jnp.where(row == col, piece, 0.0)
        total = total + jnp.sum(kept)
    return total[0:1, 0:1]


def first_step(x_ref, gram_f32, gram_ref, poly_ref, out_ref):
    width = x_ref.shape[0]
    tile = min(256, width)
    for n in range(0, width, tile):
        gram_f32[:, n : n + tile] = nt_dot(x_ref[...], x_ref[n : n + tile, :])
    squares = trace_of(gram_f32)
    inverse = 1.0 / (jnp.sqrt(squares) + norm_epsilon)
    gram_ref[...] = (gram_f32[...] * (inverse * inverse)).astype(jnp.bfloat16)
    for n in range(0, width, tile):
        square = jnp.dot(gram_ref[...], gram_ref[:, n : n + tile], preferred_element_type=jnp.float32)
        poly_ref[:, n : n + tile] = (
            newton_cubic * gram_ref[:, n : n + tile].astype(jnp.float32) + newton_quintic * square
        ).astype(jnp.bfloat16)
    for n in range(0, x_ref.shape[1], 256):
        product = jnp.dot(poly_ref[...], x_ref[:, n : n + 256], preferred_element_type=jnp.float32)
        out_ref[:, n : n + 256] = (
            (newton_linear * x_ref[:, n : n + 256].astype(jnp.float32) + product) * inverse
        ).astype(jnp.bfloat16)


def last_step(x_ref, gram_ref, own, count, main_lanes, rest_lanes):
    width = x_ref.shape[0]
    tile = min(256, width)
    for n in range(0, width, tile):
        gram_ref[:, n : n + tile] = nt_dot(x_ref[...], x_ref[n : n + tile, :]).astype(jnp.bfloat16)
    part = gram_ref[own, :]
    square = jnp.dot(part, gram_ref[...], preferred_element_type=jnp.float32)
    poly = (newton_cubic * part.astype(jnp.float32) + newton_quintic * square).astype(jnp.bfloat16)
    results = []
    for lanes in (main_lanes, rest_lanes):
        product = jnp.dot(poly, x_ref[:, lanes], preferred_element_type=jnp.float32)
        results.append(newton_linear * x_ref[own, lanes].astype(jnp.float32) + product)
    return results


def pack(block):
    groups = [block[k * REST : (k + 1) * REST, 256:320] for k in range(3)]
    groups.append(jnp.concatenate([block[BIG_W:, 256:320], jnp.zeros((REST - SMALL_W, 64), jnp.float32)], axis=0))
    return jnp.concatenate([block[:, :256], jnp.concatenate(groups, axis=1)], axis=0)


def muon_kernel(
    owners,
    big_grad_hbm,
    big_weight_hbm,
    big_moment_hbm,
    small_grad_hbm,
    small_weight_hbm,
    small_moment_hbm,
    parts_hbm,
    param,
    first,
    second,
    big_weight_new,
    big_moment_new,
    small_weight_new,
    small_moment_new,
    param_new,
    first_new,
    second_new,
    big_grad,
    big_weight,
    big_moment,
    small_grad,
    small_weight,
    small_moment,
    parts,
    load_sem,
    grad_rows,
    grad_out,
    moment_out,
    moment_in,
    blocks,
    big_x,
    big_next,
    small_x,
    small_next,
    big_gram_f32,
    big_gram,
    big_poly,
    small_gram_f32,
    small_gram,
    small_poly,
    result_rows,
    result_in,
    small_rows,
    small_in,
    parts_in,
    swap_sem,
    moment_sem,
    stage_send,
    stage_recv,
    pair_send,
    pair_recv,
    own_sem,
    back_sem,
    vec_send,
    vec_recv,
):
    loads = [
        pltpu.make_async_copy(source, target, load_sem.at[k])
        for k, (source, target) in enumerate(
            (
                (big_grad_hbm, big_grad),
                (small_grad_hbm, small_grad),
                (big_moment_hbm, big_moment),
                (small_moment_hbm, small_moment),
                (parts_hbm, parts),
                (big_weight_hbm, big_weight),
                (small_weight_hbm, small_weight),
            )
        )
    ]
    for copy in loads:
        copy.start()
    shard = lax.axis_index("shard")
    tensor = lax.axis_index("tensor")
    group = shard // 4
    place = shard % 4
    z, y = place // 2, shard % 2
    x, core = tensor // 2, tensor % 2
    partner = {"shard": (shard + 4) % 8, "tensor": tensor}
    sibling = {"shard": shard, "tensor": x * 2 + (1 - core)}
    neighbour = {
        "x": {"shard": shard, "tensor": (1 - x) * 2 + core},
        "y": {"shard": group * 4 + z * 2 + (1 - y), "tensor": tensor},
        "z": {"shard": group * 4 + (1 - z) * 2 + y, "tensor": tensor},
    }

    barrier = pltpu.get_barrier_semaphore()
    for k in range(1, 8):
        pl.semaphore_signal(
            barrier, inc=1, device_id={"shard": (shard + k) % 8, "tensor": tensor}, device_id_type=MESH
        )
    for peer in (neighbour["x"], sibling):
        pl.semaphore_signal(barrier, inc=1, device_id=peer, device_id_type=MESH)

    first_is_mine = jnp.where(owners[0, 0] >= 4, 1, 0) == group
    small_is_mine = jnp.where(owners[1, 0] >= 4, 1, 0) == group
    big_owner = lax.rem(jnp.where(first_is_mine, owners[0, 0], owners[0, 1]), 4)
    small_owner = lax.rem(jnp.where(small_is_mine, owners[1, 0], owners[1, 1]), 4)

    def columns(index):
        big = jnp.where(first_is_mine == (index == 0), big_grad[0].astype(jnp.float32), big_grad[1].astype(jnp.float32))
        small = jnp.where(
            small_is_mine == (index == 0), small_grad[0].astype(jnp.float32), small_grad[1].astype(jnp.float32)
        )
        picked = small[:, 0:SMALL_W]
        for k in range(1, 4):
            picked = jnp.where(tensor == k, small[:, k * SMALL_W : (k + 1) * SMALL_W], picked)
        filler = jnp.zeros((ROWS, 256 - BLOCK), jnp.float32)
        return jnp.concatenate([big, picked, filler], axis=1).astype(jnp.bfloat16)

    loads[0].wait()
    loads[1].wait()
    grad_out[...] = columns(1)
    pl.semaphore_wait(barrier, 9)
    own_rows = pl.ds(pl.multiple_of(group * ROWS, ROWS), ROWS)
    other_rows = pl.ds(pl.multiple_of((1 - group) * ROWS, ROWS), ROWS)
    swap = pltpu.make_async_remote_copy(
        grad_out, grad_rows.at[own_rows], swap_sem.at[0], swap_sem.at[1], device_id=partner, device_id_type=MESH
    )
    swap.start()

    loads[2].wait()
    loads[3].wait()
    moment = jnp.concatenate(
        [big_moment[0], small_moment[0, pl.ds(pl.multiple_of(tensor * SMALL_W, SMALL_W), SMALL_W), :]], axis=0
    )
    for j in range(4):
        rows = jnp.concatenate(
            [moment[:, j * ROWS : (j + 1) * ROWS], moment[:, (j + 4) * ROWS : (j + 5) * ROWS]], axis=1
        )
        moment_out[j] = pack(rows).astype(jnp.bfloat16)
    moves = []
    for k in (3, 2, 1):
        there = (place + k) % 4
        moves.append(
            pltpu.make_async_remote_copy(
                moment_out.at[there],
                moment_in.at[place],
                moment_sem.at[0, k],
                moment_sem.at[1, k],
                device_id={"shard": group * 4 + there, "tensor": tensor},
                device_id_type=MESH,
            )
        )
        moves[-1].start()
    loads[4].wait()
    vec_moves = []
    for k in range(1, 8):
        there = (shard + k) % 8
        vec_moves.append(
            pltpu.make_async_remote_copy(
                parts.at[there],
                parts_in.at[k],
                vec_send.at[k],
                vec_recv.at[k],
                device_id={"shard": there, "tensor": tensor},
                device_id_type=MESH,
            )
        )
        vec_moves[-1].start()
    moment_in[place] = moment_out[place]
    grad_rows[own_rows, :] = columns(0)
    grad_rows[2 * ROWS :, :] = jnp.zeros((LANES - 2 * ROWS, 256), jnp.bfloat16)
    swap.wait_recv()
    gradient = pack(grad_rows[...].astype(jnp.float32).T[:BLOCK])
    for move in moves:
        move.wait_recv()
    low = moment_in[big_owner, BLOCK:, :]
    high = moment_in[small_owner, BLOCK:, :]
    lane = lax.broadcasted_iota(jnp.int32, (REST, 256), 1)
    previous = jnp.concatenate(
        [
            moment_in[big_owner, :BIG_W, :].astype(jnp.float32),
            moment_in[small_owner, BIG_W:BLOCK, :].astype(jnp.float32),
            jnp.where(lane < BIG_W, low.astype(jnp.float32), high.astype(jnp.float32)),
        ],
        axis=0,
    )
    renewed = momentum_rate * previous + gradient
    blocks[z, y, x, core] = (gradient + momentum_rate * renewed).astype(jnp.bfloat16)

    here = {"x": x, "y": y, "z": z}

    def region(p, k, received):
        done = ORDERS[p][:k]
        index = []
        for name in ("z", "y", "x"):
            if name in done:
                index.append(slice(None))
            elif received and name == ORDERS[p][k]:
                index.append(1 - here[name])
            else:
                index.append(here[name])
        return blocks.at[index[0], index[1], index[2], core, pl.ds(*PARTS[p])]

    def stage(p, k):
        ref = region(p, k, False)
        return pltpu.make_async_remote_copy(
            ref,
            ref,
            stage_send.at[p, k],
            stage_recv.at[p, k],
            device_id=neighbour[ORDERS[p][k]],
            device_id_type=MESH,
        )

    def forward(p, k):
        ref = region(p, k, True)
        return pltpu.make_async_remote_copy(
            ref, ref, pair_send.at[p, k], pair_recv.at[p, k], device_id=sibling, device_id_type=MESH
        )

    sent = []
    for p in range(3):
        copy = stage(p, 0)
        copy.start()
        sent.append(copy)
    own_ref = blocks.at[z, y, x, core]
    own_copy = pltpu.make_async_remote_copy(
        own_ref, own_ref, own_sem.at[0], own_sem.at[1], device_id=sibling, device_id_type=MESH
    )
    own_copy.start()
    forwarded = []
    for k in range(3):
        for p in range(3):
            sent[3 * k + p].wait_recv()
            if k < 2:
                copy = stage(p, k + 1)
                copy.start()
                sent.append(copy)
            copy = forward(p, k)
            copy.start()
            forwarded.append(copy)
    own_copy.wait_recv()
    for copy in forwarded:
        copy.wait_recv()

    for a in range(2):
        for b in range(2):
            lanes = slice((2 * a + b) * 256, (2 * a + b + 1) * 256)
            for t in range(4):
                big_x[t * BIG_W : (t + 1) * BIG_W, lanes] = blocks[a, b, t // 2, t % 2, :BIG_W, :256]
                small_x[t * SMALL_W : (t + 1) * SMALL_W, lanes] = blocks[a, b, t // 2, t % 2, BIG_W:BLOCK, :256]
        lanes = slice(1024 + a * 128, 1024 + (a + 1) * 128)
        for t in range(4):
            left = blocks[a, 0, t // 2, t % 2, BLOCK:, :].astype(jnp.float32)
            right = blocks[a, 1, t // 2, t % 2, BLOCK:, :].astype(jnp.float32)
            for k in range(4):
                both = jnp.concatenate(
                    [left[:, k * 64 : (k + 1) * 64], right[:, k * 64 : (k + 1) * 64]], axis=1
                ).astype(jnp.bfloat16)
                if k < 3:
                    big_x[t * BIG_W + k * REST : t * BIG_W + (k + 1) * REST, lanes] = both
                else:
                    small_x[t * SMALL_W : (t + 1) * SMALL_W, lanes] = both[:SMALL_W]

    main_lanes = pl.ds(pl.multiple_of(place * 256, 256), 256)
    rest_lanes = pl.ds(pl.multiple_of(1024 + z * 128, 128), 128)

    def give_back(results, rows_ref, in_ref, sems):
        main, rest = results
        rest = jnp.where(y == 0, rest, pltpu.roll(rest, 64, 1))
        rows_ref[0:256, :] = main.T.astype(jnp.bfloat16)
        rows_ref[256:LANES, :] = rest.T.astype(jnp.bfloat16)
        copy = pltpu.make_async_remote_copy(
            rows_ref.at[other_rows], in_ref, sems.at[0], sems.at[1], device_id=partner, device_id_type=MESH
        )
        copy.start()
        return copy

    first_step(small_x, small_gram_f32, small_gram, small_poly, small_next)
    small_results = last_step(small_next, small_gram, slice(None), 4 * SMALL_W, main_lanes, rest_lanes)
    small_back = give_back(small_results, small_rows, small_in, back_sem.at[1])
    first_step(big_x, big_gram_f32, big_gram, big_poly, big_next)
    own_columns = pl.ds(pl.multiple_of(tensor * BIG_W, BIG_W), BIG_W)
    big_results = last_step(big_next, big_gram, own_columns, BIG_W, main_lanes, rest_lanes)
    back = give_back(big_results, result_rows, result_in, back_sem.at[0])

    share = parts[shard]
    for k in range(1, 8):
        vec_moves[k - 1].wait_recv()
        share = share + parts_in[k]
    first_value = first_decay * first[...] + (1.0 - first_decay) * share
    second_value = second_decay * second[...] + (1.0 - second_decay) * share * share
    first_new[...] = first_value
    second_new[...] = second_value
    param_new[...] = param[...] - adam_rate * (first_value / first_correct) / (
        jnp.sqrt(second_value / second_correct) + adam_epsilon
    )

    from_blended = 1.0 / (1.0 + momentum_rate)
    from_moment = momentum_rate - momentum_rate * momentum_rate / (1.0 + momentum_rate)

    def row_order(values):
        low, high = [], []
        for j in range(4):
            low.append(values[:, 256 * j : 256 * j + ROWS])
            high += [values[:, 256 * j + ROWS : 256 * (j + 1)], values[:, 1024 + 64 * j : 1024 + 64 * (j + 1)]]
        return jnp.concatenate(low + high, axis=1)

    big_moment_new[0] = jnp.where(
        big_owner == place,
        from_blended * row_order(big_x[own_columns, :].astype(jnp.float32)) + from_moment * big_moment[0],
        big_moment[0],
    )
    small_moment_new[0] = jnp.where(
        small_owner == place,
        from_blended * row_order(small_x[...].astype(jnp.float32)) + from_moment * small_moment[0],
        small_moment[0],
    )

    small_back.wait_recv()
    back.wait_recv()
    loads[5].wait()
    loads[6].wait()
    scale = 0.2 * math.sqrt(D)
    for index in range(2):
        for weight, out, rows_ref, in_ref, is_mine in (
            (small_weight, small_weight_new, small_rows, small_in, small_is_mine),
            (big_weight, big_weight_new, result_rows, result_in, first_is_mine),
        ):
            update = jnp.where(
                is_mine == (index == 0), rows_ref[own_rows, :].astype(jnp.float32), in_ref[...].astype(jnp.float32)
            )
            values = weight[index].astype(jnp.float32)
            out[index] = (values - muon_rate * (scale * update + weight_decay * values)).astype(jnp.bfloat16)
    for copy in [swap, own_copy, small_back, back] + moves + vec_moves + sent + forwarded:
        copy.wait_send()


def per_device(
    big_grad,
    big_weight,
    big_moment,
    small_grad,
    small_weight,
    small_moment,
    owners,
    vec_parts,
    vec_param,
    vec_first,
    vec_second,
):
    entries = vec_param.shape[0]
    shards = lax.axis_size("shard")
    vmem = pl.BlockSpec(memory_space=pltpu.VMEM)
    hbm = pl.BlockSpec(memory_space=pl.ANY)
    rows = jax.ShapeDtypeStruct((1, entries), jnp.float32)
    out_shape = (
        jax.ShapeDtypeStruct(big_weight.shape, jnp.bfloat16),
        jax.ShapeDtypeStruct(big_moment.shape, jnp.float32),
        jax.ShapeDtypeStruct(small_weight.shape, jnp.bfloat16),
        jax.ShapeDtypeStruct(small_moment.shape, jnp.float32),
        rows,
        rows,
        rows,
    )
    bf16, f32 = jnp.bfloat16, jnp.float32
    big, small = 4 * BIG_W, 4 * SMALL_W
    dma = pltpu.SemaphoreType.DMA
    outs = pl.pallas_call(
        muon_kernel,
        out_shape=out_shape,
        in_specs=[pl.BlockSpec(memory_space=pltpu.SMEM)] + [hbm] * 7 + [vmem] * 3,
        out_specs=(vmem,) * 7,
        scratch_shapes=[
            pltpu.VMEM(big_grad.shape, bf16),
            pltpu.VMEM(big_weight.shape, bf16),
            pltpu.VMEM(big_moment.shape, f32),
            pltpu.VMEM(small_grad.shape, bf16),
            pltpu.VMEM(small_weight.shape, bf16),
            pltpu.VMEM(small_moment.shape, f32),
            pltpu.VMEM((shards, 1, entries), f32),
            dma((7,)),
            pltpu.VMEM((LANES, 256), bf16),
            pltpu.VMEM((ROWS, 256), bf16),
            pltpu.VMEM((4, PACKED, 256), bf16),
            pltpu.VMEM((4, PACKED, 256), bf16),
            pltpu.VMEM((2, 2, 2, 2, PACKED, 256), bf16),
            pltpu.VMEM((big, D), bf16),
            pltpu.VMEM((big, D), bf16),
            pltpu.VMEM((small, D), bf16),
            pltpu.VMEM((small, D), bf16),
            pltpu.VMEM((big, big), f32),
            pltpu.VMEM((big, big), bf16),
            pltpu.VMEM((big, big), bf16),
            pltpu.VMEM((small, small), f32),
            pltpu.VMEM((small, small), bf16),
            pltpu.VMEM((small, small), bf16),
            pltpu.VMEM((LANES, BIG_W), bf16),
            pltpu.VMEM((ROWS, BIG_W), bf16),
            pltpu.VMEM((LANES, 4 * SMALL_W), bf16),
            pltpu.VMEM((ROWS, 4 * SMALL_W), bf16),
            pltpu.VMEM((shards, 1, entries), f32),
            dma((2,)),
            dma((2, 4)),
            dma((3, 3)),
            dma((3, 3)),
            dma((3, 3)),
            dma((3, 3)),
            dma((2,)),
            dma((2, 2)),
            dma((8,)),
            dma((8,)),
        ],
        compiler_params=pltpu.CompilerParams(
            collective_id=0, has_side_effects=True, vmem_limit_bytes=60 * 1024 * 1024
        ),
    )(
        owners,
        big_grad,
        big_weight,
        big_moment,
        small_grad,
        small_weight,
        small_moment,
        vec_parts.reshape(shards, 1, entries),
        vec_param.reshape(1, entries),
        vec_first.reshape(1, entries),
        vec_second.reshape(1, entries),
    )
    return tuple(outs[:4]) + tuple(value.reshape(entries) for value in outs[4:])


def solution(mesh):
    grouped = mesh.shape["shard"] == 8 and mesh.shape["tensor"] == 4
    return jax.shard_map(
        per_device if grouped else per_device_routed,
        mesh=mesh,
        in_specs=(
            P(None, "shard", "tensor"),
            P(None, "shard", "tensor"),
            P("shard", "tensor", None),
            P(None, "shard", None),
            P(None, "shard", None),
            P("shard", None, None),
            P(),
            P("shard", None),
            P("shard"),
            P("shard"),
            P("shard"),
        ),
        out_specs=(
            P(None, "shard", "tensor"),
            P("shard", "tensor", None),
            P(None, "shard", None),
            P("shard", None, None),
            P("shard"),
            P("shard"),
            P("shard"),
        ),
        check_vma=False,
    )
```
